256 devices in a mesh: outer: 32 (over x, z), inner: 8 (over y, core).
Axes of the slice: x: 4, y: 4, z: 8, core: 2. Of those that a mesh axis runs over, the one named last changes fastest.
Arguments:
- queries: bfloat16 [131072, 512], P(('outer', 'inner')), may hold values from -96 to 96
- keys: bfloat16 [131072, 128], P(('outer', 'inner')), may hold values from -4 to 4
- values: bfloat16 [131072, 128], P(('outer', 'inner')), may hold values from -6 to 6
- selected: int32 [128, 3], replicated, may hold values from -1 to 126, as said below
- out_weight: bfloat16 [512, 4096], replicated, may hold values from -2 to 2
Outputs:
- projected: bfloat16 [131072, 4096], P(('outer', 'inner'))
The draws below stay inside these ranges and needn't reach their ends.
Inputs may be any that keep to these rules, and one draw needn't show every extreme that they name: `selected`: row b lists key blocks for query block b: entry 0 is b - 1 (or -1 for b = 0); the other entries are distinct blocks below b - 1, or -1 where fewer than 2 such blocks exist. -1 marks an absent block.
All inputs are finite; a program needn't handle non-finite values.
Results may differ from the reference program's by a relative error of at most 0.0052.
Values may be sent and summed in bfloat16 or wider, within the bound.
No kernel may reach another device: no remote copies, remote signals or barrier semaphores. Data moves between devices by JAX's collectives and lax.ppermute only.
A program may use at most 64 MiB of HBM per device.

```python
import math
import jax
import jax.numpy as jnp
from jax import lax

D = 4096
HD = 128
HEADS = 4
BLOCK = 1024
SEL = 3
TOKENS = 131072
NBLK = 128


def shared_rows(key):
    return jnp.clip(jax.random.normal(key, (TOKENS, HD), jnp.float32), -4.0, 4.0)


def draw_keys(key, part):
    key_rows = shared_rows(key)
    return key_rows.astype(jnp.bfloat16)


def draw_queries(key, part):
    key = jax.random.fold_in(key, 5)
    query_rows = 2.0 * jnp.clip(jax.random.normal(key, (TOKENS, HEADS * HD), jnp.float32), -4.0, 4.0)
    return query_rows.astype(jnp.bfloat16)


def draw_selected(key, part):
    key = jax.random.fold_in(key, 7)
    row_ids = jnp.arange(NBLK, dtype=jnp.int32)[:, None]
    column_ids = jnp.arange(NBLK, dtype=jnp.int32)[None, :]
    priority = jax.random.randint(key, (NBLK, NBLK), 0, 1 << 20, dtype=jnp.int32) * NBLK + column_ids
    priority = jnp.where(column_ids <= row_ids - 2, priority, -1 - column_ids)
    chosen = lax.top_k(priority, SEL - 1)[1].astype(jnp.int32)
    others = jnp.where(chosen <= row_ids - 2, chosen, -1)
    neighbour = jnp.where(row_ids >= 1, row_ids - 1, -1)
    return jnp.concatenate([neighbour, others], axis=1).astype(jnp.int32)


def block_scale(rng, extent, pieces, low, high):
    def one(axis_at, parts):
        draws = jax.random.uniform(jax.random.fold_in(jax.random.fold_in(rng, 6), axis_at), (parts,), jnp.float32, low / len(pieces), high / len(pieces))
        return jnp.repeat(jnp.exp(draws), extent[axis_at] // parts).reshape((-1,) + (1,) * (len(extent) - axis_at - 1))

    level = one(*pieces[0])
    for cut in pieces[1:]:
        level = level * one(*cut)
    return level


def bell_draw(own_key, dims, spread, most, split=(), kind=jnp.bfloat16):
    gain = block_scale(own_key, dims, split, -0.22, 0.18) if split else 1.0
    values = jax.random.normal(own_key, dims, jnp.float32) * spread * gain
    return jnp.minimum(jnp.maximum(values, -most), most).astype(kind)


def setup_inputs(seed: int = 0) -> dict:
    streams_of = jax.random.split(jax.random.key(seed), 6)
    queries = draw_queries(jax.random.fold_in(streams_of[5], 71), 0)
    keys = draw_keys(jax.random.fold_in(streams_of[5], 71), 0)
    values = bell_draw(streams_of[2], (TOKENS, HD), 1.0, 6.0, ((0, 256),))
    selected = draw_selected(jax.random.fold_in(streams_of[5], 71), 0)
    out_weight = bell_draw(streams_of[4], (HEADS * HD, D), (HEADS * HD // 64) ** -0.5, 2.0)
    return {"queries": queries, "keys": keys, "values": values, "selected": selected, "out_weight": out_weight}


def group_terms(q_heads, key_rows, value_rows, causal, score_scale):
    scores = jnp.einsum('rhd,kd->hrk', q_heads.astype(jnp.float32), key_rows.astype(jnp.float32)) * score_scale
    scores = jnp.where(causal[None, :, :], scores, -jnp.inf)
    maxima = lax.optimization_barrier(jnp.max(scores, axis=-1))
    powers = jnp.exp(scores - maxima[:, :, None])
    totals = lax.optimization_barrier(jnp.sum(powers, axis=-1))
    weights = lax.optimization_barrier(powers.astype(jnp.bfloat16)).astype(jnp.float32)
    outputs = jnp.einsum('hrk,kd->hrd', weights, value_rows.astype(jnp.float32))
    return (maxima, totals, outputs)

def combine(groups, present, out_weight, row_count):
    maxima = jnp.stack([group[0] for group in groups])
    totals = jnp.stack([group[1] for group in groups])
    outputs = jnp.stack([group[2] for group in groups])
    present = jnp.stack(present)[:, None, None]
    largest = lax.optimization_barrier(jnp.max(jnp.where(present, maxima, -jnp.inf), axis=0))
    factors = jnp.where(present, jnp.exp(maxima - largest[None]), 0.0)
    numerator = lax.optimization_barrier(jnp.sum(factors[..., None] * outputs, axis=0))
    denominator = lax.optimization_barrier(jnp.sum(factors * totals, axis=0))
    attended = jnp.transpose(numerator / denominator[:, :, None], (1, 0, 2)).reshape(row_count, -1).astype(jnp.bfloat16)
    return jnp.dot(attended, out_weight, preferred_element_type=jnp.float32).astype(jnp.bfloat16)

def reference(queries, keys, values, selected, out_weight):
    score_scale = 1.0 / math.sqrt(HD)
    positions = jnp.arange(BLOCK, dtype=jnp.int32)
    causal = positions[None, :] <= positions[:, None]
    open_mask = jnp.ones((BLOCK, BLOCK), dtype=bool)

    def one_block(block_index):
        row_start = (block_index * BLOCK).astype(jnp.int32)
        q_heads = lax.dynamic_slice_in_dim(queries, row_start, BLOCK, 0).reshape(BLOCK, HEADS, HD)
        own_keys = lax.dynamic_slice_in_dim(keys, row_start, BLOCK, 0)
        own_values = lax.dynamic_slice_in_dim(values, row_start, BLOCK, 0)
        groups = [group_terms(q_heads, own_keys, own_values, causal, score_scale)]
        present = [jnp.ones((), dtype=bool)]
        for slot_index in range(SEL):
            listed = selected[block_index, slot_index]
            key_start = (jnp.maximum(listed, 0) * BLOCK).astype(jnp.int32)
            far_keys = lax.dynamic_slice_in_dim(keys, key_start, BLOCK, 0)
            far_values = lax.dynamic_slice_in_dim(values, key_start, BLOCK, 0)
            groups.append(group_terms(q_heads, far_keys, far_values, open_mask, score_scale))
            present.append(listed >= 0)
        return combine(groups, present, out_weight, BLOCK)
    blocks_out = lax.map(one_block, jnp.arange(NBLK, dtype=jnp.int32))
    return blocks_out.reshape(TOKENS, D)
```

```python
import math

import jax
import jax.numpy as jnp
from jax import lax
from jax.experimental import pallas as pl
from jax.experimental.pallas import tpu as pltpu
from jax.sharding import Mesh
from jax.sharding import PartitionSpec as P

HEADS = 4
HD = 128
HALF = 512
CHIPS = 128
PIECE = 8
FREE = 2
LOG2E = 1.4426950408889634
SCALE = LOG2E / math.sqrt(HD)
NEG = -1e30
ROWS = 256
OUT_COLS = 1024
CHIP_AXES = ("outer", "ring")
ALL_AXES = ("outer", "ring", "core")


def dot_t(a, b):
    return lax.dot_general(a, b, (((1,), (1,)), ((), ())), preferred_element_type=jnp.float32)


def with_ones(values):
    return jnp.concatenate([values, jnp.ones_like(values)], axis=1)


def near_kernel(where_ref, q_ref, own_ref, pair_ref, nb_ref, nbx_ref, acc_ref, ml_ref):
    block = where_ref[0]
    core = where_ref[1]
    own_bias = jnp.where(core == 1, 0.0, NEG)
    near_bias = jnp.where(block >= 1, 0.0, NEG)
    row_ids = lax.broadcasted_iota(jnp.int32, (ROWS, HALF), 0)
    col_ids = lax.broadcasted_iota(jnp.int32, (ROWS, HALF), 1)
    vs = [with_ones(ref[HALF:, :]) for ref in (own_ref, pair_ref, nb_ref, nbx_ref)]
    for head in range(HEADS):
        for part in range(HALF // ROWS):
            rows = pl.ds(part * ROWS, ROWS)
            q = q_ref[rows, head * HD:(head + 1) * HD]
            s_own = dot_t(q, own_ref[:HALF, :])
            s_own = jnp.where(col_ids <= row_ids + part * ROWS, s_own, NEG)
            scores = [
                s_own,
                dot_t(q, pair_ref[:HALF, :]) + own_bias,
                dot_t(q, nb_ref[:HALF, :]) + near_bias,
                dot_t(q, nbx_ref[:HALF, :]) + near_bias,
            ]
            top = scores[0]
            for s in scores[1:]:
                top = jnp.maximum(top, s)
            m = jnp.max(top, axis=1, keepdims=True)
            out = jnp.zeros((ROWS, 2 * HD), jnp.float32)
            for s, v in zip(scores, vs):
                p = jnp.exp2((s - m) * SCALE).astype(jnp.bfloat16)
                out = out + jnp.dot(p, v, preferred_element_type=jnp.float32)
            acc_ref[rows, head * HD:(head + 1) * HD] = out[:, :HD]
            ml_ref[rows, head:head + 1] = m
            ml_ref[rows, HEADS + head:HEADS + head + 1] = out[:, HD:HD + 1]


def near_groups(where, queries, own, pair, near, near_pair):
    vmem = pl.BlockSpec(memory_space=pltpu.VMEM)
    return pl.pallas_call(
        near_kernel,
        out_shape=(
            jax.ShapeDtypeStruct((HALF, HEADS * HD), jnp.float32),
            jax.ShapeDtypeStruct((HALF, 2 * HEADS), jnp.float32),
        ),
        in_specs=[pl.BlockSpec(memory_space=pltpu.SMEM)] + [vmem] * 5,
        out_specs=(vmem, vmem),
        cost_estimate=pl.CostEstimate(
            flops=4 * 2 * 2048 * 2048 * 128, bytes_accessed=4 << 20, transcendentals=2048 * 2048
        ),
        compiler_params=pltpu.CompilerParams(vmem_limit_bytes=40 << 20),
    )(where, queries, own, pair, near, near_pair)


def pick_kernel(listed_ref, pieces_ref, out_ref):
    def step(at, carry):
        for slot in range(FREE):
            block = jnp.maximum(listed_ref[1 + slot, at], 0)
            out_ref[FREE * at + slot] = pieces_ref[block]
        return carry

    lax.fori_loop(0, CHIPS, step, 0, unroll=8)


def pick_pieces(listed, pieces):
    vmem = pl.BlockSpec(memory_space=pltpu.VMEM)
    return pl.pallas_call(
        pick_kernel,
        out_shape=jax.ShapeDtypeStruct((CHIPS * FREE, PIECE, HD), jnp.bfloat16),
        in_specs=[pl.BlockSpec(memory_space=pltpu.SMEM), vmem],
        out_specs=vmem,
        cost_estimate=pl.CostEstimate(flops=0, bytes_accessed=1 << 20, transcendentals=0),
    )(listed, pieces)


def far_kernel(where_ref, q_ref, far_ref, farx_ref, acc_ref, ml_ref, w_ref, out_ref, att_ref):
    @pl.when(pl.program_id(0) == 0)
    def _():
        keys = 2 * HALF
        parity = (lax.broadcasted_iota(jnp.int32, (1, keys), 1) // PIECE) % FREE
        bias = jnp.where(
            parity == 0,
            jnp.where(where_ref[2] >= 0, 0.0, NEG),
            jnp.where(where_ref[3] >= 0, 0.0, NEG),
        )
        vs = [with_ones(ref[keys:, :]) for ref in (far_ref, farx_ref)]
        for head in range(HEADS):
            for part in range(HALF // ROWS):
                rows = pl.ds(part * ROWS, ROWS)
                q = q_ref[rows, head * HD:(head + 1) * HD]
                scores = [dot_t(q, ref[:keys, :]) + bias for ref in (far_ref, farx_ref)]
                old = ml_ref[rows, head:head + 1]
                m = jnp.max(jnp.maximum(scores[0], scores[1]), axis=1, keepdims=True)
                m = jnp.maximum(m, old)
                keep = jnp.exp2((old - m) * SCALE)
                out = jnp.zeros((ROWS, 2 * HD), jnp.float32)
                for s, v in zip(scores, vs):
                    p = jnp.exp2((s - m) * SCALE).astype(jnp.bfloat16)
                    out = out + jnp.dot(p, v, preferred_element_type=jnp.float32)
                total = out[:, HD:] + keep * ml_ref[rows, HEADS + head:HEADS + head + 1]
                top = out[:, :HD] + keep * acc_ref[rows, head * HD:(head + 1) * HD]
                att_ref[rows, head * HD:(head + 1) * HD] = (top / total).astype(jnp.bfloat16)

    out_ref[...] = jnp.dot(
        att_ref[...], w_ref[...], preferred_element_type=jnp.float32
    ).astype(out_ref.dtype)


def far_groups(where, queries, far, far_pair, acc, ml, out_weight):
    width = out_weight.shape[1]

    def whole(array):
        return pl.BlockSpec(array.shape, lambda i: (0,) * array.ndim, pipeline_mode=pl.Buffered(1))

    return pl.pallas_call(
        far_kernel,
        grid=(width // OUT_COLS,),
        out_shape=jax.ShapeDtypeStruct((HALF, width), jnp.bfloat16),
        in_specs=[pl.BlockSpec(memory_space=pltpu.SMEM)]
        + [whole(a) for a in (queries, far, far_pair, acc, ml)]
        + [pl.BlockSpec((HEADS * HD, OUT_COLS), lambda i: (0, i))],
        out_specs=pl.BlockSpec((HALF, OUT_COLS), lambda i: (0, i)),
        scratch_shapes=[pltpu.VMEM((HALF, HEADS * HD), jnp.bfloat16)],
        cost_estimate=pl.CostEstimate(
            flops=4 * 2 * 2048 * 2048 * 128 + 2 * 512 * 512 * 4096,
            bytes_accessed=12 << 20,
            transcendentals=2048 * 2048,
        ),
        compiler_params=pltpu.CompilerParams(vmem_limit_bytes=40 << 20),
    )(where, queries, far, far_pair, acc, ml, out_weight)


def swap_cores(value):
    return lax.ppermute(value, "core", [(0, 1), (1, 0)])


def local(queries, keys, values, selected, out_weight):
    listed = selected.T
    block = lax.axis_index(CHIP_AXES)
    core = lax.axis_index("core")
    mine = lax.dynamic_index_in_dim(selected, block, 0, keepdims=False)
    where = jnp.stack([block, core, mine[1], mine[2]]).astype(jnp.int32)
    own = jnp.concatenate([keys, values], axis=0)

    pieces = lax.all_to_all(
        own.reshape(CHIPS, PIECE, HD), CHIP_AXES, split_axis=0, concat_axis=0, tiled=True
    )
    outgoing = pick_pieces(listed, pieces)
    far = lax.all_to_all(outgoing, CHIP_AXES, split_axis=0, concat_axis=0, tiled=True)
    far = far.reshape(CHIPS * FREE * PIECE, HD)
    far_pair = swap_cores(far)

    near = lax.ppermute(own, CHIP_AXES, [(i, i + 1) for i in range(CHIPS - 1)])
    acc, ml = near_groups(where, queries, own, swap_cores(own), near, swap_cores(near))
    return far_groups(where, queries, far, far_pair, acc, ml, out_weight)


def solution(mesh):
    outer, inner = mesh.devices.shape
    fine = Mesh(mesh.devices.reshape(outer, inner // 2, 2), ALL_AXES)
    tokens = P(ALL_AXES, None)
    return jax.shard_map(
        local,
        mesh=fine,
        in_specs=(tokens, tokens, tokens, P(), P()),
        out_specs=tokens,
        check_vma=False,
    )
```

```python
import math

import jax
import jax.numpy as jnp
from jax import lax
from jax.experimental import pallas as pl
from jax.experimental.pallas import tpu as pltpu
from jax.sharding import Mesh
from jax.sharding import PartitionSpec as P

HEADS = 4
HD = 128
HALF = 512
CHIPS = 128
PIECE = 8
FREE = 2
LOG2E = 1.4426950408889634
SCALE = LOG2E / math.sqrt(HD)
NEG = -1e30
ROWS = 256
OUT_COLS = 2048
CHIP_AXES = ("outer", "ring")
ALL_AXES = ("outer", "ring", "core")


def dot_t(a, b):
    return lax.dot_general(a, b, (((1,), (1,)), ((), ())), preferred_element_type=jnp.float32)


def with_ones(values):
    return jnp.concatenate([values, jnp.ones_like(values)], axis=1)


def in_hbm(array):
    return pltpu.with_memory_space_constraint(array, pltpu.HBM)


def near_kernel(q_hbm, own_ref, pair_ref, nb_ref, nbx_ref, acc_ref, ml_ref, q_ref, sem):
    q_copy = pltpu.make_async_copy(q_hbm, q_ref, sem)
    q_copy.start()
    block = lax.axis_index(CHIP_AXES)
    core = lax.axis_index("core")
    own_bias = jnp.where(core == 1, 0.0, NEG)
    near_bias = jnp.where(block >= 1, 0.0, NEG)
    row_ids = lax.broadcasted_iota(jnp.int32, (ROWS, HALF), 0)
    col_ids = lax.broadcasted_iota(jnp.int32, (ROWS, HALF), 1)
    vs = [with_ones(ref[HALF:, :]) for ref in (own_ref, pair_ref, nb_ref, nbx_ref)]
    q_copy.wait()
    for part in range(HALF // ROWS):
        for head in range(HEADS):
            rows = slice(part * ROWS, (part + 1) * ROWS)
            q = q_ref[rows, head * HD:(head + 1) * HD]
            s_own = dot_t(q, own_ref[:HALF, :])
            s_own = jnp.where(col_ids <= row_ids + part * ROWS, s_own, NEG)
            scores = [
                s_own,
                dot_t(q, pair_ref[:HALF, :]) + own_bias,
                dot_t(q, nb_ref[:HALF, :]) + near_bias,
                dot_t(q, nbx_ref[:HALF, :]) + near_bias,
            ]
            top = scores[0]
            for s in scores[1:]:
                top = jnp.maximum(top, s)
            m = jnp.max(top, axis=1, keepdims=True)
            out = jnp.zeros((ROWS, 2 * HD), jnp.float32)
            for s, v in zip(scores, vs):
                p = jnp.exp2((s - m) * SCALE).astype(jnp.bfloat16)
                out = out + jnp.dot(p, v, preferred_element_type=jnp.float32)
            acc_ref[rows, head * HD:(head + 1) * HD] = out[:, :HD]
            ml_ref[rows, head:head + 1] = m
            ml_ref[rows, HEADS + head:HEADS + head + 1] = out[:, HD:HD + 1]


def near_groups(queries, own, pair, near, near_pair):
    vmem = pl.BlockSpec(memory_space=pltpu.VMEM)
    return pl.pallas_call(
        near_kernel,
        out_shape=(
            pltpu.VMEM((HALF, HEADS * HD), jnp.float32),
            pltpu.VMEM((HALF, 2 * HEADS), jnp.float32),
            pltpu.VMEM(queries.shape, queries.dtype),
        ),
        in_specs=[pl.BlockSpec(memory_space=pltpu.HBM)] + [vmem] * 4,
        out_specs=[vmem] * 3,
        scratch_shapes=[pltpu.SemaphoreType.DMA],
        cost_estimate=pl.CostEstimate(
            flops=4 * 2 * 2048 * 2048 * 128, bytes_accessed=4 << 20, transcendentals=2048 * 2048
        ),
        compiler_params=pltpu.CompilerParams(vmem_limit_bytes=20 << 20),
    )(in_hbm(queries), own, pair, near, near_pair)


def join_kernel(keys_ref, values_ref, out_ref, sems):
    rows = keys_ref.shape[0]
    copies = [
        pltpu.make_async_copy(ref, out_ref.at[pl.ds(at * rows, rows)], sems.at[at])
        for at, ref in enumerate((keys_ref, values_ref))
    ]
    for copy in copies:
        copy.start()
    for copy in copies:
        copy.wait()


def join(keys, values):
    return pl.pallas_call(
        join_kernel,
        out_shape=pltpu.VMEM((2 * keys.shape[0], keys.shape[1]), keys.dtype),
        in_specs=[pl.BlockSpec(memory_space=pltpu.HBM)] * 2,
        out_specs=pl.BlockSpec(memory_space=pltpu.VMEM),
        scratch_shapes=[pltpu.SemaphoreType.DMA((2,))],
        compiler_params=pltpu.CompilerParams(vmem_limit_bytes=2 << 20),
    )(in_hbm(keys), in_hbm(values))


def pick_kernel(listed_ref, pieces_ref, *rest):
    out_ref = rest[-1]

    def step(at, carry):
        for slot in range(FREE):
            block = jnp.maximum(listed_ref[1 + slot, at], 0)
            out_ref[FREE * at + slot] = pieces_ref[block]
        return carry

    lax.fori_loop(0, CHIPS, step, 0, unroll=32)


def pick_pieces(listed, pieces, *ready):
    vmem = pl.BlockSpec(memory_space=pltpu.VMEM)
    return pl.pallas_call(
        pick_kernel,
        out_shape=pltpu.VMEM((CHIPS * FREE, PIECE, HD), jnp.bfloat16),
        in_specs=[pl.BlockSpec(memory_space=pltpu.SMEM), vmem] + [vmem] * len(ready),
        out_specs=vmem,
        cost_estimate=pl.CostEstimate(flops=0, bytes_accessed=1 << 20, transcendentals=0),
        compiler_params=pltpu.CompilerParams(vmem_limit_bytes=2 << 20),
    )(in_hbm(listed), pieces, *ready)


def far_kernel(listed_ref, q_ref, far_ref, farx_ref, acc_ref, ml_ref, w_hbm, out_hbm, att_ref, out_ref, w_ref, sems, w_sem):
    w_copy = pltpu.make_async_copy(w_hbm, w_ref, w_sem)
    w_copy.start()
    keys = 2 * HALF
    width = w_ref.shape[1]
    block = lax.axis_index(CHIP_AXES)
    parity = (lax.broadcasted_iota(jnp.int32, (1, keys), 1) // PIECE) % FREE
    bias = jnp.where(
        parity == 0,
        jnp.where(listed_ref[1, block] >= 0, 0.0, NEG),
        jnp.where(listed_ref[2, block] >= 0, 0.0, NEG),
    )
    vs = [with_ones(ref[keys:, :]) for ref in (far_ref, farx_ref)]
    copies = []
    for part in range(HALF // ROWS):
        rows = slice(part * ROWS, (part + 1) * ROWS)
        for head in range(HEADS):
            q = q_ref[rows, head * HD:(head + 1) * HD]
            scores = [dot_t(q, ref[:keys, :]) + bias for ref in (far_ref, farx_ref)]
            old = ml_ref[rows, head:head + 1]
            m = jnp.max(jnp.maximum(scores[0], scores[1]), axis=1, keepdims=True)
            m = jnp.maximum(m, old)
            keep = jnp.exp2((old - m) * SCALE)
            out = jnp.zeros((ROWS, 2 * HD), jnp.float32)
            for s, v in zip(scores, vs):
                p = jnp.exp2((s - m) * SCALE).astype(jnp.bfloat16)
                out = out + jnp.dot(p, v, preferred_element_type=jnp.float32)
            total = out[:, HD:] + keep * ml_ref[rows, HEADS + head:HEADS + head + 1]
            top = out[:, :HD] + keep * acc_ref[rows, head * HD:(head + 1) * HD]
            att_ref[rows, head * HD:(head + 1) * HD] = (top / total).astype(jnp.bfloat16)
        if part == 0:
            w_copy.wait()
        for start in range(0, width, OUT_COLS):
            cols = slice(start, start + OUT_COLS)
            out_ref[rows, cols] = jnp.dot(
                att_ref[rows, :], w_ref[:, cols], preferred_element_type=jnp.float32
            ).astype(out_ref.dtype)
            at = (pl.ds(part * ROWS, ROWS), pl.ds(start, OUT_COLS))
            copies.append(
                pltpu.make_async_copy(out_ref.at[at], out_hbm.at[at], sems.at[len(copies)])
            )
            copies[-1].start()
    for copy in copies:
        copy.wait()


def far_groups(listed, queries, far, far_pair, acc, ml, out_weight):
    width = out_weight.shape[1]
    vmem = pl.BlockSpec(memory_space=pltpu.VMEM)
    return pl.pallas_call(
        far_kernel,
        out_shape=jax.ShapeDtypeStruct((HALF, width), jnp.bfloat16),
        in_specs=[pl.BlockSpec(memory_space=pltpu.SMEM)] + [vmem] * 5
        + [pl.BlockSpec(memory_space=pltpu.HBM)],
        out_specs=pl.BlockSpec(memory_space=pltpu.HBM),
        scratch_shapes=[
            pltpu.VMEM((HALF, HEADS * HD), jnp.bfloat16),
            pltpu.VMEM((HALF, width), jnp.bfloat16),
            pltpu.VMEM(out_weight.shape, jnp.bfloat16),
            pltpu.SemaphoreType.DMA((HALF // ROWS * (width // OUT_COLS),)),
            pltpu.SemaphoreType.DMA,
        ],
        cost_estimate=pl.CostEstimate(
            flops=4 * 2 * 2048 * 2048 * 128 + 2 * 512 * 512 * 4096,
            bytes_accessed=12 << 20,
            transcendentals=2048 * 2048,
        ),
        compiler_params=pltpu.CompilerParams(vmem_limit_bytes=20 << 20),
    )(in_hbm(listed), queries, far, far_pair, acc, ml, in_hbm(out_weight))


def swap_cores(value):
    return lax.ppermute(value, "core", [(0, 1), (1, 0)])


def local(queries, keys, values, selected, out_weight):
    listed = selected.T
    own = join(keys, values)
    pieces = lax.all_to_all(
        own.reshape(CHIPS, PIECE, HD), CHIP_AXES, split_axis=0, concat_axis=0, tiled=True
    )
    near = lax.ppermute(own, CHIP_AXES, [(i, i + 1) for i in range(CHIPS - 1)])
    near_pair = swap_cores(near)
    own_pair = swap_cores(own)
    outgoing = pick_pieces(listed, pieces, own_pair, near, near_pair)
    far = lax.all_to_all(outgoing, CHIP_AXES, split_axis=0, concat_axis=0, tiled=True)
    far = far.reshape(CHIPS * FREE * PIECE, HD)
    acc, ml, queries = near_groups(queries, own, own_pair, near, near_pair)
    far, acc, ml = lax.optimization_barrier((far, acc, ml))
    far_pair = swap_cores(far)
    return far_groups(listed, queries, far, far_pair, acc, ml, out_weight)


def solution(mesh):
    outer, inner = mesh.devices.shape
    fine = Mesh(mesh.devices.reshape(outer, inner // 2, 2), ALL_AXES)
    tokens = P(ALL_AXES, None)
    return jax.shard_map(
        local,
        mesh=fine,
        in_specs=(tokens, tokens, tokens, P(), P()),
        out_specs=tokens,
        check_vma=False,
    )
```

```python
import functools
import math

import jax
import jax.numpy as jnp
from jax import lax
from jax.experimental import pallas as pl
from jax.experimental.pallas import tpu as pltpu
from jax.sharding import Mesh
from jax.sharding import PartitionSpec as P

HEADS = 4
HD = 128
HALF = 512
CHIPS = 128
PIECE = 8
FREE = 2
LOG2E = 1.4426950408889634
SCALE = LOG2E / math.sqrt(HD)
NEG = -1e30
ROWS = 256
OUT_COLS = 2048
CHIP_AXES = ("outer", "ring")
ALL_AXES = ("outer", "ring", "core")


def dot_t(a, b):
    return lax.dot_general(a, b, (((1,), (1,)), ((), ())), preferred_element_type=jnp.float32)


def with_ones(values):
    return jnp.concatenate([values, jnp.ones_like(values)], axis=1)


def weighted(scores, values, m):
    out = None
    for s, v in zip(scores, values):
        p = jnp.exp2((s - m) * SCALE).astype(jnp.bfloat16)
        term = jnp.dot(p, v, preferred_element_type=jnp.float32)
        out = term if out is None else out + term
    return out


def in_hbm(array):
    return pltpu.with_memory_space_constraint(array, pltpu.HBM)


def near_kernel(q_hbm, own_ref, pair_ref, nb_ref, nbx_ref, acc_ref, ml_ref, q_ref, sem):
    q_copy = pltpu.make_async_copy(q_hbm, q_ref, sem)
    q_copy.start()
    block = lax.axis_index(CHIP_AXES)
    core = lax.axis_index("core")
    own_bias = jnp.where(core == 1, 0.0, NEG)
    near_bias = jnp.where(block >= 1, 0.0, NEG)
    row_ids = lax.broadcasted_iota(jnp.int32, (ROWS, HALF), 0)
    col_ids = lax.broadcasted_iota(jnp.int32, (ROWS, HALF), 1)
    vs = [with_ones(ref[HALF:, :]) for ref in (own_ref, pair_ref, nb_ref, nbx_ref)]
    q_copy.wait()

    def scores_of(step):
        part, head = divmod(step, HEADS)
        q = q_ref[part * ROWS:(part + 1) * ROWS, head * HD:(head + 1) * HD]
        own = jnp.where(
            col_ids <= row_ids + part * ROWS, dot_t(q, own_ref[:HALF, :]), NEG
        )
        return [
            own,
            dot_t(q, pair_ref[:HALF, :]) + own_bias,
            dot_t(q, nb_ref[:HALF, :]) + near_bias,
            dot_t(q, nbx_ref[:HALF, :]) + near_bias,
        ]

    steps = HALF // ROWS * HEADS
    later = scores_of(0)
    for step in range(steps):
        part, head = divmod(step, HEADS)
        rows = slice(part * ROWS, (part + 1) * ROWS)
        scores = later
        later = scores_of(step + 1) if step + 1 < steps else None
        m = jnp.max(functools.reduce(jnp.maximum, scores), axis=1, keepdims=True)
        out = weighted(scores, vs, m)
        acc_ref[rows, head * HD:(head + 1) * HD] = out[:, :HD]
        ml_ref[rows, head:head + 1] = m
        ml_ref[rows, HEADS + head:HEADS + head + 1] = out[:, HD:HD + 1]


def near_groups(queries, own, pair, near, near_pair):
    vmem = pl.BlockSpec(memory_space=pltpu.VMEM)
    return pl.pallas_call(
        near_kernel,
        out_shape=(
            pltpu.VMEM((HALF, HEADS * HD), jnp.float32),
            pltpu.VMEM((HALF, 2 * HEADS), jnp.float32),
            pltpu.VMEM(queries.shape, queries.dtype),
        ),
        in_specs=[pl.BlockSpec(memory_space=pltpu.HBM)] + [vmem] * 4,
        out_specs=[vmem] * 3,
        scratch_shapes=[pltpu.SemaphoreType.DMA],
        cost_estimate=pl.CostEstimate(
            flops=4 * 2 * 2048 * 2048 * 128, bytes_accessed=4 << 20, transcendentals=2048 * 2048
        ),
        compiler_params=pltpu.CompilerParams(vmem_limit_bytes=20 << 20),
    )(in_hbm(queries), own, pair, near, near_pair)


def join_kernel(keys_ref, values_ref, out_ref, sems):
    rows = keys_ref.shape[0]
    copies = [
        pltpu.make_async_copy(ref, out_ref.at[pl.ds(at * rows, rows)], sems.at[at])
        for at, ref in enumerate((keys_ref, values_ref))
    ]
    for copy in copies:
        copy.start()
    for copy in copies:
        copy.wait()


def join(keys, values):
    return pl.pallas_call(
        join_kernel,
        out_shape=pltpu.VMEM((2 * keys.shape[0], keys.shape[1]), keys.dtype),
        in_specs=[pl.BlockSpec(memory_space=pltpu.HBM)] * 2,
        out_specs=pl.BlockSpec(memory_space=pltpu.VMEM),
        scratch_shapes=[pltpu.SemaphoreType.DMA((2,))],
        compiler_params=pltpu.CompilerParams(vmem_limit_bytes=2 << 20),
    )(in_hbm(keys), in_hbm(values))


def pick_kernel(listed_ref, pieces_ref, *rest):
    out_ref = rest[-1]

    def step(at, carry):
        for slot in range(FREE):
            block = jnp.maximum(listed_ref[1 + slot, at], 0)
            out_ref[FREE * at + slot] = pieces_ref[block]
        return carry

    lax.fori_loop(0, CHIPS, step, 0, unroll=32)


def pick_pieces(listed, pieces, *ready):
    vmem = pl.BlockSpec(memory_space=pltpu.VMEM)
    return pl.pallas_call(
        pick_kernel,
        out_shape=pltpu.VMEM((CHIPS * FREE, PIECE, HD), jnp.bfloat16),
        in_specs=[pl.BlockSpec(memory_space=pltpu.SMEM), vmem] + [vmem] * len(ready),
        out_specs=vmem,
        cost_estimate=pl.CostEstimate(flops=0, bytes_accessed=1 << 20, transcendentals=0),
        compiler_params=pltpu.CompilerParams(vmem_limit_bytes=2 << 20),
    )(in_hbm(listed), pieces, *ready)


def far_kernel(listed_ref, q_ref, far_ref, farx_ref, acc_ref, ml_ref, w_hbm, out_hbm, att_ref, out_ref, w_ref, sems, w_sem):
    w_copy = pltpu.make_async_copy(w_hbm, w_ref, w_sem)
    w_copy.start()
    keys = 2 * HALF
    width = w_ref.shape[1]
    block = lax.axis_index(CHIP_AXES)
    parity = (lax.broadcasted_iota(jnp.int32, (1, keys), 1) // PIECE) % FREE
    bias = jnp.where(
        parity == 0,
        jnp.where(listed_ref[1, block] >= 0, 0.0, NEG),
        jnp.where(listed_ref[2, block] >= 0, 0.0, NEG),
    )
    vs = [with_ones(ref[keys:, :]) for ref in (far_ref, farx_ref)]
    copies = []

    def scores_of(step):
        part, head = divmod(step, HEADS)
        q = q_ref[part * ROWS:(part + 1) * ROWS, head * HD:(head + 1) * HD]
        return [dot_t(q, ref[:keys, :]) + bias for ref in (far_ref, farx_ref)]

    def project(part):
        rows = slice(part * ROWS, (part + 1) * ROWS)
        if part == 0:
            w_copy.wait()
        for start in range(0, width, OUT_COLS):
            cols = slice(start, start + OUT_COLS)
            out_ref[rows, cols] = jnp.dot(
                att_ref[rows, :], w_ref[:, cols], preferred_element_type=jnp.float32
            ).astype(out_ref.dtype)
            at = (pl.ds(part * ROWS, ROWS), pl.ds(start, OUT_COLS))
            copies.append(
                pltpu.make_async_copy(out_ref.at[at], out_hbm.at[at], sems.at[len(copies)])
            )
            copies[-1].start()

    parts = HALF // ROWS
    later = scores_of(0)
    for step in range(parts * HEADS):
        part, head = divmod(step, HEADS)
        rows = slice(part * ROWS, (part + 1) * ROWS)
        scores = later
        later = scores_of(step + 1) if step + 1 < parts * HEADS else None
        if head == 0 and part > 0:
            project(part - 1)
        old = ml_ref[rows, head:head + 1]
        m = jnp.maximum(jnp.max(jnp.maximum(*scores), axis=1, keepdims=True), old)
        keep = jnp.exp2((old - m) * SCALE)
        out = weighted(scores, vs, m)
        total = out[:, HD:] + keep * ml_ref[rows, HEADS + head:HEADS + head + 1]
        top = out[:, :HD] + keep * acc_ref[rows, head * HD:(head + 1) * HD]
        att_ref[rows, head * HD:(head + 1) * HD] = (top / total).astype(jnp.bfloat16)
    project(parts - 1)
    for copy in copies:
        copy.wait()


def far_groups(listed, queries, far, far_pair, acc, ml, out_weight):
    width = out_weight.shape[1]
    vmem = pl.BlockSpec(memory_space=pltpu.VMEM)
    return pl.pallas_call(
        far_kernel,
        out_shape=jax.ShapeDtypeStruct((HALF, width), jnp.bfloat16),
        in_specs=[pl.BlockSpec(memory_space=pltpu.SMEM)] + [vmem] * 5
        + [pl.BlockSpec(memory_space=pltpu.HBM)],
        out_specs=pl.BlockSpec(memory_space=pltpu.HBM),
        scratch_shapes=[
            pltpu.VMEM((HALF, HEADS * HD), jnp.bfloat16),
            pltpu.VMEM((HALF, width), jnp.bfloat16),
            pltpu.VMEM(out_weight.shape, jnp.bfloat16),
            pltpu.SemaphoreType.DMA((HALF // ROWS * (width // OUT_COLS),)),
            pltpu.SemaphoreType.DMA,
        ],
        cost_estimate=pl.CostEstimate(
            flops=4 * 2 * 2048 * 2048 * 128 + 2 * 512 * 512 * 4096,
            bytes_accessed=12 << 20,
            transcendentals=2048 * 2048,
        ),
        compiler_params=pltpu.CompilerParams(vmem_limit_bytes=20 << 20),
    )(in_hbm(listed), queries, far, far_pair, acc, ml, in_hbm(out_weight))


def swap_cores(value):
    return lax.ppermute(value, "core", [(0, 1), (1, 0)])


def local(queries, keys, values, selected, out_weight):
    listed = selected.T
    own = join(keys, values)
    pieces = lax.all_to_all(
        own.reshape(CHIPS, PIECE, HD), CHIP_AXES, split_axis=0, concat_axis=0, tiled=True
    )
    near = lax.ppermute(own, CHIP_AXES, [(i, (i + 1) % CHIPS) for i in range(CHIPS)])
    near_pair = swap_cores(near)
    own_pair = swap_cores(own)
    outgoing = pick_pieces(listed, pieces, own_pair, near, near_pair)
    far = lax.all_to_all(outgoing, CHIP_AXES, split_axis=0, concat_axis=0, tiled=True)
    far = far.reshape(CHIPS * FREE * PIECE, HD)
    acc, ml, queries = near_groups(queries, own, own_pair, near, near_pair)
    far, acc, ml = lax.optimization_barrier((far, acc, ml))
    far_pair = swap_cores(far)
    return far_groups(listed, queries, far, far_pair, acc, ml, out_weight)


def solution(mesh):
    outer, inner = mesh.devices.shape
    fine = Mesh(mesh.devices.reshape(outer, inner // 2, 2), ALL_AXES)
    tokens = P(ALL_AXES, None)
    return jax.shard_map(
        local,
        mesh=fine,
        in_specs=(tokens, tokens, tokens, P(), P()),
        out_specs=tokens,
        check_vma=False,
    )
```

```python
import functools
import math

import jax
import jax.numpy as jnp
from jax import lax
from jax.experimental import pallas as pl
from jax.experimental.pallas import tpu as pltpu
from jax.sharding import Mesh
from jax.sharding import PartitionSpec as P

HEADS = 4
HD = 128
HALF = 512
CHIPS = 128
PIECE = 8
FREE = 2
LOG2E = 1.4426950408889634
SCALE = LOG2E / math.sqrt(HD)
NEG = -1e30
ROWS = 256
OUT_COLS = 2048
PICK_PARTS = 4
CHIP_AXES = ("outer", "ring")
ALL_AXES = ("outer", "ring", "core")


def dot_t(a, b):
    return lax.dot_general(a, b, (((1,), (1,)), ((), ())), preferred_element_type=jnp.float32)


def with_ones(values):
    return jnp.concatenate([values, jnp.ones_like(values)], axis=1)


def weighted(scores, values, m):
    out = None
    for s, v in zip(scores, values):
        p = jnp.exp2((s - m) * SCALE).astype(jnp.bfloat16)
        term = jnp.dot(p, v, preferred_element_type=jnp.float32)
        out = term if out is None else out + term
    return out


def in_hbm(array):
    return pltpu.with_memory_space_constraint(array, pltpu.HBM)


def near_kernel(listed_ref, q_hbm, own_ref, pair_ref, nb_ref, nbx_ref, acc_ref, ml_ref, q_ref, bias_ref, sem):
    q_copy = pltpu.make_async_copy(q_hbm, q_ref, sem)
    q_copy.start()
    block = lax.axis_index(CHIP_AXES)
    core = lax.axis_index("core")
    parity = (lax.broadcasted_iota(jnp.int32, (8, 2 * HALF), 1) // PIECE) % FREE
    bias_ref[...] = jnp.where(
        parity == 0,
        jnp.where(listed_ref[1, block] >= 0, 0.0, NEG),
        jnp.where(listed_ref[2, block] >= 0, 0.0, NEG),
    )
    own_bias = jnp.where(core == 1, 0.0, NEG)
    near_bias = jnp.where(block >= 1, 0.0, NEG)
    row_ids = lax.broadcasted_iota(jnp.int32, (ROWS, HALF), 0)
    col_ids = lax.broadcasted_iota(jnp.int32, (ROWS, HALF), 1)
    vs = [with_ones(ref[HALF:, :]) for ref in (own_ref, pair_ref, nb_ref, nbx_ref)]
    q_copy.wait()

    def scores_of(step):
        part, head = divmod(step, HEADS)
        q = q_ref[part * ROWS:(part + 1) * ROWS, head * HD:(head + 1) * HD]
        own = jnp.where(
            col_ids <= row_ids + part * ROWS, dot_t(q, own_ref[:HALF, :]), NEG
        )
        return [
            own,
            dot_t(q, pair_ref[:HALF, :]) + own_bias,
            dot_t(q, nb_ref[:HALF, :]) + near_bias,
            dot_t(q, nbx_ref[:HALF, :]) + near_bias,
        ]

    steps = HALF // ROWS * HEADS
    later = scores_of(0)
    for step in range(steps):
        part, head = divmod(step, HEADS)
        rows = slice(part * ROWS, (part + 1) * ROWS)
        scores = later
        later = scores_of(step + 1) if step + 1 < steps else None
        m = jnp.max(functools.reduce(jnp.maximum, scores), axis=1, keepdims=True)
        out = weighted(scores, vs, m)
        acc_ref[rows, head * HD:(head + 1) * HD] = out[:, :HD]
        ml_ref[rows, head:head + 1] = m
        ml_ref[rows, HEADS + head:HEADS + head + 1] = out[:, HD:HD + 1]


def near_groups(listed, queries, own, pair, near, near_pair):
    vmem = pl.BlockSpec(memory_space=pltpu.VMEM)
    return pl.pallas_call(
        near_kernel,
        out_shape=(
            pltpu.VMEM((HALF, HEADS * HD), jnp.float32),
            pltpu.VMEM((HALF, 2 * HEADS), jnp.float32),
            pltpu.VMEM(queries.shape, queries.dtype),
            pltpu.VMEM((8, 2 * HALF), jnp.float32),
        ),
        in_specs=[
            pl.BlockSpec(memory_space=pltpu.SMEM),
            pl.BlockSpec(memory_space=pltpu.HBM),
        ]
        + [vmem] * 4,
        out_specs=[vmem] * 4,
        scratch_shapes=[pltpu.SemaphoreType.DMA],
        cost_estimate=pl.CostEstimate(
            flops=4 * 2 * 2048 * 2048 * 128, bytes_accessed=4 << 20, transcendentals=2048 * 2048
        ),
        compiler_params=pltpu.CompilerParams(vmem_limit_bytes=20 << 20),
    )(listed, in_hbm(queries), own, pair, near, near_pair)


def join_kernel(keys_ref, values_ref, listed_ref, out_ref, table_ref, held_ref, sems):
    rows = keys_ref.shape[0]
    parts = [pl.ds(at * rows, rows) for at in range(2)]
    table = pltpu.make_async_copy(listed_ref, table_ref, sems.at[4])
    inward = [
        pltpu.make_async_copy(ref, held_ref.at[part], sems.at[at])
        for at, (ref, part) in enumerate(zip((keys_ref, values_ref), parts))
    ]
    outward = [
        pltpu.make_async_copy(held_ref.at[part], out_ref.at[part], sems.at[2 + at])
        for at, part in enumerate(parts)
    ]
    for copy in inward:
        copy.start()
    table.start()
    for first, second in zip(inward, outward):
        first.wait()
        second.start()
    for copy in outward:
        copy.wait()
    table.wait()


def join(keys, values, listed):
    hbm = pl.BlockSpec(memory_space=pltpu.HBM)
    shape = (2 * keys.shape[0], keys.shape[1])
    return pl.pallas_call(
        join_kernel,
        out_shape=(
            jax.ShapeDtypeStruct(shape, keys.dtype),
            pltpu.SMEM(listed.shape, listed.dtype),
        ),
        in_specs=[hbm] * 3,
        out_specs=(hbm, pl.BlockSpec(memory_space=pltpu.SMEM)),
        scratch_shapes=[pltpu.VMEM(shape, keys.dtype), pltpu.SemaphoreType.DMA((5,))],
        compiler_params=pltpu.CompilerParams(vmem_limit_bytes=2 << 20),
    )(in_hbm(keys), in_hbm(values), in_hbm(listed))


def pick_kernel(listed_ref, pieces_ref, *rest):
    out_hbm, out_ref, sems = rest[-3:]

    def step(at, carry):
        for slot in range(FREE):
            block = jnp.maximum(listed_ref[1 + slot, at], 0)
            out_ref[FREE * at + slot] = pieces_ref[block]
        return carry

    copies = []
    each = CHIPS // PICK_PARTS
    for part in range(PICK_PARTS):
        lax.fori_loop(part * each, (part + 1) * each, step, 0, unroll=True)
        at = pl.ds(part * each * FREE, each * FREE)
        copies.append(pltpu.make_async_copy(out_ref.at[at], out_hbm.at[at], sems.at[part]))
        copies[-1].start()
    for copy in copies:
        copy.wait()


def pick_pieces(listed, pieces, *ready):
    vmem = pl.BlockSpec(memory_space=pltpu.VMEM)
    shape = (CHIPS * FREE, PIECE, HD)
    return pl.pallas_call(
        pick_kernel,
        out_shape=jax.ShapeDtypeStruct(shape, jnp.bfloat16),
        in_specs=[pl.BlockSpec(memory_space=pltpu.SMEM), vmem] + [vmem] * len(ready),
        out_specs=pl.BlockSpec(memory_space=pltpu.HBM),
        scratch_shapes=[pltpu.VMEM(shape, jnp.bfloat16), pltpu.SemaphoreType.DMA((PICK_PARTS,))],
        cost_estimate=pl.CostEstimate(flops=0, bytes_accessed=1 << 20, transcendentals=0),
        compiler_params=pltpu.CompilerParams(vmem_limit_bytes=2 << 20),
    )(listed, pieces, *ready)


def far_kernel(bias_ref, q_ref, far_ref, farx_ref, acc_ref, ml_ref, w_hbm, out_hbm, att_ref, out_ref, w_ref, sems, w_sem):
    w_copy = pltpu.make_async_copy(w_hbm, w_ref, w_sem)
    w_copy.start()
    keys = 2 * HALF
    width = w_ref.shape[1]
    bias = bias_ref[0:1, :]
    vs = [with_ones(ref[keys:, :]) for ref in (far_ref, farx_ref)]
    copies = []

    def scores_of(step):
        part, head = divmod(step, HEADS)
        q = q_ref[part * ROWS:(part + 1) * ROWS, head * HD:(head + 1) * HD]
        return [dot_t(q, ref[:keys, :]) + bias for ref in (far_ref, farx_ref)]

    def project(part):
        rows = slice(part * ROWS, (part + 1) * ROWS)
        if part == 0:
            w_copy.wait()
        for start in range(0, width, OUT_COLS):
            cols = slice(start, start + OUT_COLS)
            out_ref[rows, cols] = jnp.dot(
                att_ref[rows, :], w_ref[:, cols], preferred_element_type=jnp.float32
            ).astype(out_ref.dtype)
            at = (pl.ds(part * ROWS, ROWS), pl.ds(start, OUT_COLS))
            copies.append(
                pltpu.make_async_copy(out_ref.at[at], out_hbm.at[at], sems.at[len(copies)])
            )
            copies[-1].start()

    parts = HALF // ROWS
    later = scores_of(0)
    for step in range(parts * HEADS):
        part, head = divmod(step, HEADS)
        rows = slice(part * ROWS, (part + 1) * ROWS)
        scores = later
        later = scores_of(step + 1) if step + 1 < parts * HEADS else None
        if head == 0 and part > 0:
            project(part - 1)
        old = ml_ref[rows, head:head + 1]
        m = jnp.maximum(jnp.max(jnp.maximum(*scores), axis=1, keepdims=True), old)
        keep = jnp.exp2((old - m) * SCALE)
        out = weighted(scores, vs, m)
        total = out[:, HD:] + keep * ml_ref[rows, HEADS + head:HEADS + head + 1]
        top = out[:, :HD] + keep * acc_ref[rows, head * HD:(head + 1) * HD]
        att_ref[rows, head * HD:(head + 1) * HD] = (top / total).astype(jnp.bfloat16)
    project(parts - 1)
    for copy in copies:
        copy.wait()


def far_groups(bias, queries, far, far_pair, acc, ml, out_weight):
    width = out_weight.shape[1]
    vmem = pl.BlockSpec(memory_space=pltpu.VMEM)
    return pl.pallas_call(
        far_kernel,
        out_shape=jax.ShapeDtypeStruct((HALF, width), jnp.bfloat16),
        in_specs=[vmem] * 6
        + [pl.BlockSpec(memory_space=pltpu.HBM)],
        out_specs=pl.BlockSpec(memory_space=pltpu.HBM),
        scratch_shapes=[
            pltpu.VMEM((HALF, HEADS * HD), jnp.bfloat16),
            pltpu.VMEM((HALF, width), jnp.bfloat16),
            pltpu.VMEM(out_weight.shape, jnp.bfloat16),
            pltpu.SemaphoreType.DMA((HALF // ROWS * (width // OUT_COLS),)),
            pltpu.SemaphoreType.DMA,
        ],
        cost_estimate=pl.CostEstimate(
            flops=4 * 2 * 2048 * 2048 * 128 + 2 * 512 * 512 * 4096,
            bytes_accessed=12 << 20,
            transcendentals=2048 * 2048,
        ),
        compiler_params=pltpu.CompilerParams(vmem_limit_bytes=20 << 20),
    )(bias, queries, far, far_pair, acc, ml, in_hbm(out_weight))


def swap_cores(value):
    return lax.ppermute(value, "core", [(0, 1), (1, 0)])


def local(queries, keys, values, selected, out_weight):
    listed = selected.T
    own, table = join(keys, values, listed)
    pieces = lax.all_to_all(
        own.reshape(CHIPS, PIECE, HD), CHIP_AXES, split_axis=0, concat_axis=0, tiled=True
    )
    near = lax.ppermute(own, CHIP_AXES, [(i, (i + 1) % CHIPS) for i in range(CHIPS)])
    near_pair = swap_cores(near)
    own_pair = swap_cores(own)
    outgoing = pick_pieces(table, pieces, own_pair, near, near_pair)
    far = lax.all_to_all(outgoing, CHIP_AXES, split_axis=0, concat_axis=0, tiled=True)
    far = far.reshape(CHIPS * FREE * PIECE, HD)
    acc, ml, queries, bias = near_groups(table, queries, own, own_pair, near, near_pair)
    far, acc, ml = lax.optimization_barrier((far, acc, ml))
    far_pair = swap_cores(far)
    return far_groups(bias, queries, far, far_pair, acc, ml, out_weight)


def solution(mesh):
    outer, inner = mesh.devices.shape
    fine = Mesh(mesh.devices.reshape(outer, inner // 2, 2), ALL_AXES)
    tokens = P(ALL_AXES, None)
    return jax.shard_map(
        local,
        mesh=fine,
        in_specs=(tokens, tokens, tokens, P(), P()),
        out_specs=tokens,
        check_vma=False,
    )
```

```python
import functools
import math

import jax
import jax.numpy as jnp
from jax import lax
from jax.experimental import pallas as pl
from jax.experimental.pallas import tpu as pltpu
from jax.sharding import Mesh
from jax.sharding import PartitionSpec as P

HEADS = 4
HD = 128
HALF = 512
CHIPS = 128
PIECE = 8
FREE = 2
LOG2E = 1.4426950408889634
SCALE = LOG2E / math.sqrt(HD)
NEG = -1e30
ROWS = 256
OUT_COLS = 1024
PICK_PARTS = 4
CHIP_AXES = ("outer", "ring")
ALL_AXES = ("outer", "ring", "core")


def dot_t(a, b):
    return lax.dot_general(a, b, (((1,), (1,)), ((), ())), preferred_element_type=jnp.float32)


def with_ones(values):
    return jnp.concatenate([values, jnp.ones_like(values)], axis=1)


def weighted(scores, values, m):
    out = None
    for s, v in zip(scores, values):
        p = jnp.exp2((s - m) * SCALE).astype(jnp.bfloat16)
        term = jnp.dot(p, v, preferred_element_type=jnp.float32)
        out = term if out is None else out + term
    return out


def in_hbm(array):
    return pltpu.with_memory_space_constraint(array, pltpu.HBM)


def near_kernel(listed_ref, q_hbm, own_ref, pair_ref, nb_ref, nbx_ref, acc_ref, ml_ref, q_ref, bias_ref, sem):
    q_copy = pltpu.make_async_copy(q_hbm, q_ref, sem)
    q_copy.start()
    block = lax.axis_index(CHIP_AXES)
    core = lax.axis_index("core")
    parity = (lax.broadcasted_iota(jnp.int32, (8, 2 * HALF), 1) // PIECE) % FREE
    bias_ref[...] = jnp.where(
        parity == 0,
        jnp.where(listed_ref[1, block] >= 0, 0.0, NEG),
        jnp.where(listed_ref[2, block] >= 0, 0.0, NEG),
    )
    own_bias = jnp.where(core == 1, 0.0, NEG)
    near_bias = jnp.where(block >= 1, 0.0, NEG)
    row_ids = lax.broadcasted_iota(jnp.int32, (ROWS, HALF), 0)
    col_ids = lax.broadcasted_iota(jnp.int32, (ROWS, HALF), 1)
    vs = [with_ones(ref[HALF:, :]) for ref in (own_ref, pair_ref, nb_ref, nbx_ref)]
    q_copy.wait()

    def scores_of(step):
        part, head = divmod(step, HEADS)
        q = q_ref[part * ROWS:(part + 1) * ROWS, head * HD:(head + 1) * HD]
        own = jnp.where(
            col_ids <= row_ids + part * ROWS, dot_t(q, own_ref[:HALF, :]), NEG
        )
        return [
            own,
            dot_t(q, pair_ref[:HALF, :]) + own_bias,
            dot_t(q, nb_ref[:HALF, :]) + near_bias,
            dot_t(q, nbx_ref[:HALF, :]) + near_bias,
        ]

    steps = HALF // ROWS * HEADS
    later = scores_of(0)
    for step in range(steps):
        part, head = divmod(step, HEADS)
        rows = slice(part * ROWS, (part + 1) * ROWS)
        scores = later
        later = scores_of(step + 1) if step + 1 < steps else None
        m = jnp.max(functools.reduce(jnp.maximum, scores), axis=1, keepdims=True)
        out = weighted(scores, vs, m)
        acc_ref[rows, head * HD:(head + 1) * HD] = out[:, :HD]
        ml_ref[rows, head:head + 1] = m
        ml_ref[rows, HEADS + head:HEADS + head + 1] = out[:, HD:HD + 1]


def near_groups(listed, queries, own, pair, near, near_pair):
    vmem = pl.BlockSpec(memory_space=pltpu.VMEM)
    return pl.pallas_call(
        near_kernel,
        out_shape=(
            pltpu.VMEM((HALF, HEADS * HD), jnp.float32),
            pltpu.VMEM((HALF, 2 * HEADS), jnp.float32),
            pltpu.VMEM(queries.shape, queries.dtype),
            pltpu.VMEM((8, 2 * HALF), jnp.float32),
        ),
        in_specs=[
            pl.BlockSpec(memory_space=pltpu.SMEM),
            pl.BlockSpec(memory_space=pltpu.HBM),
        ]
        + [vmem] * 4,
        out_specs=[vmem] * 4,
        scratch_shapes=[pltpu.SemaphoreType.DMA],
        cost_estimate=pl.CostEstimate(
            flops=4 * 2 * 2048 * 2048 * 128, bytes_accessed=4 << 20, transcendentals=2048 * 2048
        ),
        compiler_params=pltpu.CompilerParams(vmem_limit_bytes=20 << 20),
    )(listed, in_hbm(queries), own, pair, near, near_pair)


def join_kernel(keys_ref, values_ref, listed_ref, out_ref, table_ref, held_ref, sems):
    rows = keys_ref.shape[0]
    parts = [pl.ds(at * rows, rows) for at in range(2)]
    table = pltpu.make_async_copy(listed_ref, table_ref, sems.at[4])
    inward = [
        pltpu.make_async_copy(ref, held_ref.at[part], sems.at[at])
        for at, (ref, part) in enumerate(zip((keys_ref, values_ref), parts))
    ]
    outward = [
        pltpu.make_async_copy(held_ref.at[part], out_ref.at[part], sems.at[2 + at])
        for at, part in enumerate(parts)
    ]
    for copy in inward:
        copy.start()
    table.start()
    for first, second in zip(inward, outward):
        first.wait()
        second.start()
    for copy in outward:
        copy.wait()
    table.wait()


def join(keys, values, listed):
    hbm = pl.BlockSpec(memory_space=pltpu.HBM)
    shape = (2 * keys.shape[0], keys.shape[1])
    return pl.pallas_call(
        join_kernel,
        out_shape=(
            jax.ShapeDtypeStruct(shape, keys.dtype),
            pltpu.SMEM(listed.shape, listed.dtype),
        ),
        in_specs=[hbm] * 3,
        out_specs=(hbm, pl.BlockSpec(memory_space=pltpu.SMEM)),
        scratch_shapes=[pltpu.VMEM(shape, keys.dtype), pltpu.SemaphoreType.DMA((5,))],
        compiler_params=pltpu.CompilerParams(vmem_limit_bytes=2 << 20),
    )(in_hbm(keys), in_hbm(values), in_hbm(listed))


def pick_kernel(listed_ref, pieces_ref, *rest):
    out_hbm, out_ref, sems = rest[-3:]

    def step(at, carry):
        for slot in range(FREE):
            block = jnp.maximum(listed_ref[1 + slot, at], 0)
            out_ref[FREE * at + slot] = pieces_ref[block]
        return carry

    copies = []
    each = CHIPS // PICK_PARTS
    for part in range(PICK_PARTS):
        lax.fori_loop(part * each, (part + 1) * each, step, 0, unroll=True)
        at = pl.ds(part * each * FREE, each * FREE)
        copies.append(pltpu.make_async_copy(out_ref.at[at], out_hbm.at[at], sems.at[part]))
        copies[-1].start()
    for copy in copies:
        copy.wait()


def pick_pieces(listed, pieces, *ready):
    vmem = pl.BlockSpec(memory_space=pltpu.VMEM)
    shape = (CHIPS * FREE, PIECE, HD)
    return pl.pallas_call(
        pick_kernel,
        out_shape=jax.ShapeDtypeStruct(shape, jnp.bfloat16),
        in_specs=[pl.BlockSpec(memory_space=pltpu.SMEM), vmem] + [vmem] * len(ready),
        out_specs=pl.BlockSpec(memory_space=pltpu.HBM),
        scratch_shapes=[pltpu.VMEM(shape, jnp.bfloat16), pltpu.SemaphoreType.DMA((PICK_PARTS,))],
        cost_estimate=pl.CostEstimate(flops=0, bytes_accessed=1 << 20, transcendentals=0),
        compiler_params=pltpu.CompilerParams(vmem_limit_bytes=2 << 20),
    )(listed, pieces, *ready)


def head_rows(step):
    return slice(step * ROWS, (step + 1) * ROWS)


def listed_scores(step, q_ref, far_ref, bias):
    part, head = divmod(step, HEADS)
    q = q_ref[part * ROWS:(part + 1) * ROWS, head * HD:(head + 1) * HD]
    return dot_t(q, far_ref[:far_ref.shape[0] // 2, :]) + bias


def half_kernel(bias_ref, q_ref, far_ref, scores_ref):
    bias = bias_ref[0:1, :]
    for step in range(HALF // ROWS * HEADS):
        scores_ref[head_rows(step), :] = listed_scores(step, q_ref, far_ref, bias)


def half_scores(bias, queries, far):
    vmem = pl.BlockSpec(memory_space=pltpu.VMEM)
    return pl.pallas_call(
        half_kernel,
        out_shape=pltpu.VMEM((HEADS * HALF, 2 * HALF), jnp.float32),
        in_specs=[vmem] * 3,
        out_specs=vmem,
        cost_estimate=pl.CostEstimate(
            flops=2 * 2048 * 1024 * 128, bytes_accessed=1 << 20, transcendentals=0
        ),
        compiler_params=pltpu.CompilerParams(vmem_limit_bytes=8 << 20),
    )(bias, queries, far)


def far_kernel(bias_ref, q_ref, half_ref, far_ref, farx_ref, acc_ref, ml_ref, w_hbm, out_hbm, att_ref, out_ref, w_ref, sems, w_sem):
    w_copy = pltpu.make_async_copy(w_hbm, w_ref, w_sem)
    w_copy.start()
    keys = 2 * HALF
    width = w_ref.shape[1]
    bias = bias_ref[0:1, :]
    vs = [with_ones(ref[keys:, :]) for ref in (far_ref, farx_ref)]
    copies = []

    def scores_of(step):
        return [half_ref[head_rows(step), :], listed_scores(step, q_ref, farx_ref, bias)]

    def project(part):
        rows = slice(part * ROWS, (part + 1) * ROWS)
        if part == 0:
            w_copy.wait()
        for start in range(0, width, OUT_COLS):
            cols = slice(start, start + OUT_COLS)
            out_ref[rows, cols] = jnp.dot(
                att_ref[rows, :], w_ref[:, cols], preferred_element_type=jnp.float32
            ).astype(out_ref.dtype)
            at = (pl.ds(part * ROWS, ROWS), pl.ds(start, OUT_COLS))
            copies.append(
                pltpu.make_async_copy(out_ref.at[at], out_hbm.at[at], sems.at[len(copies)])
            )
            copies[-1].start()

    parts = HALF // ROWS
    later = scores_of(0)
    for step in range(parts * HEADS):
        part, head = divmod(step, HEADS)
        rows = slice(part * ROWS, (part + 1) * ROWS)
        scores = later
        later = scores_of(step + 1) if step + 1 < parts * HEADS else None
        if head == 0 and part > 0:
            project(part - 1)
        old = ml_ref[rows, head:head + 1]
        m = jnp.maximum(jnp.max(jnp.maximum(*scores), axis=1, keepdims=True), old)
        keep = jnp.exp2((old - m) * SCALE)
        out = weighted(scores, vs, m)
        total = out[:, HD:] + keep * ml_ref[rows, HEADS + head:HEADS + head + 1]
        top = out[:, :HD] + keep * acc_ref[rows, head * HD:(head + 1) * HD]
        att_ref[rows, head * HD:(head + 1) * HD] = (top / total).astype(jnp.bfloat16)
    project(parts - 1)
    for copy in copies:
        copy.wait()


def far_groups(bias, queries, half, far, far_pair, acc, ml, out_weight):
    width = out_weight.shape[1]
    vmem = pl.BlockSpec(memory_space=pltpu.VMEM)
    return pl.pallas_call(
        far_kernel,
        out_shape=jax.ShapeDtypeStruct((HALF, width), jnp.bfloat16),
        in_specs=[vmem] * 7
        + [pl.BlockSpec(memory_space=pltpu.HBM)],
        out_specs=pl.BlockSpec(memory_space=pltpu.HBM),
        scratch_shapes=[
            pltpu.VMEM((HALF, HEADS * HD), jnp.bfloat16),
            pltpu.VMEM((HALF, width), jnp.bfloat16),
            pltpu.VMEM(out_weight.shape, jnp.bfloat16),
            pltpu.SemaphoreType.DMA((HALF // ROWS * (width // OUT_COLS),)),
            pltpu.SemaphoreType.DMA,
        ],
        cost_estimate=pl.CostEstimate(
            flops=4 * 2 * 2048 * 2048 * 128 + 2 * 512 * 512 * 4096,
            bytes_accessed=12 << 20,
            transcendentals=2048 * 2048,
        ),
        compiler_params=pltpu.CompilerParams(vmem_limit_bytes=20 << 20),
    )(bias, queries, half, far, far_pair, acc, ml, in_hbm(out_weight))


def swap_cores(value):
    return lax.ppermute(value, "core", [(0, 1), (1, 0)])


def local(queries, keys, values, selected, out_weight):
    listed = selected.T
    own, table = join(keys, values, listed)
    pieces = lax.all_to_all(
        own.reshape(CHIPS, PIECE, HD), CHIP_AXES, split_axis=0, concat_axis=0, tiled=True
    )
    near = lax.ppermute(own, CHIP_AXES, [(i, (i + 1) % CHIPS) for i in range(CHIPS)])
    near_pair = swap_cores(near)
    own_pair = swap_cores(own)
    outgoing = pick_pieces(table, pieces, own_pair, near, near_pair)
    far = lax.all_to_all(outgoing, CHIP_AXES, split_axis=0, concat_axis=0, tiled=True)
    far = far.reshape(CHIPS * FREE * PIECE, HD)
    acc, ml, queries, bias = near_groups(table, queries, own, own_pair, near, near_pair)
    far, acc, ml = lax.optimization_barrier((far, acc, ml))
    far_pair = swap_cores(far)
    half = half_scores(bias, queries, far)
    return far_groups(bias, queries, half, far, far_pair, acc, ml, out_weight)


def solution(mesh):
    outer, inner = mesh.devices.shape
    fine = Mesh(mesh.devices.reshape(outer, inner // 2, 2), ALL_AXES)
    tokens = P(ALL_AXES, None)
    return jax.shard_map(
        local,
        mesh=fine,
        in_specs=(tokens, tokens, tokens, P(), P()),
        out_specs=tokens,
        check_vma=False,
    )
```

```python
import functools
import math

import jax
import jax.numpy as jnp
from jax import lax
from jax.experimental import pallas as pl
from jax.experimental.pallas import tpu as pltpu
from jax.sharding import Mesh
from jax.sharding import PartitionSpec as P

HEADS = 4
HD = 128
HALF = 512
CHIPS = 128
PIECE = 8
FREE = 2
LOG2E = 1.4426950408889634
SCALE = LOG2E / math.sqrt(HD)
NEG = -1e30
ROWS = 256
OUT_COLS = 1024
PICK_PARTS = 4
AHEAD = 4
CHIP_AXES = ("outer", "ring")
ALL_AXES = ("outer", "ring", "core")


def dot_t(a, b):
    return lax.dot_general(a, b, (((1,), (1,)), ((), ())), preferred_element_type=jnp.float32)


def with_ones(values):
    return jnp.concatenate([values, jnp.ones_like(values)], axis=1)


def weighted(scores, values, m):
    out = None
    for s, v in zip(scores, values):
        p = jnp.exp2((s - m) * SCALE).astype(jnp.bfloat16)
        term = jnp.dot(p, v, preferred_element_type=jnp.float32)
        out = term if out is None else out + term
    return out


def in_hbm(array):
    return pltpu.with_memory_space_constraint(array, pltpu.HBM)


def near_kernel(listed_ref, q_hbm, own_ref, pair_ref, nb_ref, nbx_ref, acc_ref, ml_ref, q_ref, bias_ref, sem):
    q_copy = pltpu.make_async_copy(q_hbm, q_ref, sem)
    q_copy.start()
    block = lax.axis_index(CHIP_AXES)
    core = lax.axis_index("core")
    parity = (lax.broadcasted_iota(jnp.int32, (8, 2 * HALF), 1) // PIECE) % FREE
    bias_ref[...] = jnp.where(
        parity == 0,
        jnp.where(listed_ref[1, block] >= 0, 0.0, NEG),
        jnp.where(listed_ref[2, block] >= 0, 0.0, NEG),
    )
    own_bias = jnp.where(core == 1, 0.0, NEG)
    near_bias = jnp.where(block >= 1, 0.0, NEG)
    row_ids = lax.broadcasted_iota(jnp.int32, (ROWS, HALF), 0)
    col_ids = lax.broadcasted_iota(jnp.int32, (ROWS, HALF), 1)
    vs = [with_ones(ref[HALF:, :]) for ref in (own_ref, pair_ref, nb_ref, nbx_ref)]
    q_copy.wait()

    def scores_of(step):
        part, head = divmod(step, HEADS)
        q = q_ref[part * ROWS:(part + 1) * ROWS, head * HD:(head + 1) * HD]
        own = jnp.where(
            col_ids <= row_ids + part * ROWS, dot_t(q, own_ref[:HALF, :]), NEG
        )
        return [
            own,
            dot_t(q, pair_ref[:HALF, :]) + own_bias,
            dot_t(q, nb_ref[:HALF, :]) + near_bias,
            dot_t(q, nbx_ref[:HALF, :]) + near_bias,
        ]

    steps = HALF // ROWS * HEADS
    later = scores_of(0)
    for step in range(steps):
        part, head = divmod(step, HEADS)
        rows = slice(part * ROWS, (part + 1) * ROWS)
        scores = later
        later = scores_of(step + 1) if step + 1 < steps else None
        m = jnp.max(functools.reduce(jnp.maximum, scores), axis=1, keepdims=True)
        out = weighted(scores, vs, m)
        acc_ref[rows, head * HD:(head + 1) * HD] = out[:, :HD]
        ml_ref[rows, head:head + 1] = m
        ml_ref[rows, HEADS + head:HEADS + head + 1] = out[:, HD:HD + 1]


def near_groups(listed, queries, own, pair, near, near_pair):
    vmem = pl.BlockSpec(memory_space=pltpu.VMEM)
    return pl.pallas_call(
        near_kernel,
        out_shape=(
            pltpu.VMEM((HALF, HEADS * HD), jnp.float32),
            pltpu.VMEM((HALF, 2 * HEADS), jnp.float32),
            pltpu.VMEM(queries.shape, queries.dtype),
            pltpu.VMEM((8, 2 * HALF), jnp.float32),
        ),
        in_specs=[
            pl.BlockSpec(memory_space=pltpu.SMEM),
            pl.BlockSpec(memory_space=pltpu.HBM),
        ]
        + [vmem] * 4,
        out_specs=[vmem] * 4,
        scratch_shapes=[pltpu.SemaphoreType.DMA],
        cost_estimate=pl.CostEstimate(
            flops=4 * 2 * 2048 * 2048 * 128, bytes_accessed=4 << 20, transcendentals=2048 * 2048
        ),
        compiler_params=pltpu.CompilerParams(vmem_limit_bytes=20 << 20),
    )(listed, in_hbm(queries), own, pair, near, near_pair)


def join_kernel(keys_ref, values_ref, listed_ref, out_ref, table_ref, held_ref, sems):
    rows = keys_ref.shape[0]
    parts = [pl.ds(at * rows, rows) for at in range(2)]
    table = pltpu.make_async_copy(listed_ref, table_ref, sems.at[4])
    inward = [
        pltpu.make_async_copy(ref, held_ref.at[part], sems.at[at])
        for at, (ref, part) in enumerate(zip((keys_ref, values_ref), parts))
    ]
    outward = [
        pltpu.make_async_copy(held_ref.at[part], out_ref.at[part], sems.at[2 + at])
        for at, part in enumerate(parts)
    ]
    for copy in inward:
        copy.start()
    table.start()
    for first, second in zip(inward, outward):
        first.wait()
        second.start()
    for copy in outward:
        copy.wait()
    table.wait()


def join(keys, values, listed):
    hbm = pl.BlockSpec(memory_space=pltpu.HBM)
    shape = (2 * keys.shape[0], keys.shape[1])
    return pl.pallas_call(
        join_kernel,
        out_shape=(
            jax.ShapeDtypeStruct(shape, keys.dtype),
            pltpu.SMEM(listed.shape, listed.dtype),
        ),
        in_specs=[hbm] * 3,
        out_specs=(hbm, pl.BlockSpec(memory_space=pltpu.SMEM)),
        scratch_shapes=[pltpu.VMEM(shape, keys.dtype), pltpu.SemaphoreType.DMA((5,))],
        compiler_params=pltpu.CompilerParams(vmem_limit_bytes=2 << 20),
    )(in_hbm(keys), in_hbm(values), in_hbm(listed))


def pick_kernel(listed_ref, pieces_ref, *rest):
    out_hbm, out_ref, sems = rest[-3:]

    def step(at, carry):
        for slot in range(FREE):
            block = jnp.maximum(listed_ref[1 + slot, at], 0)
            out_ref[FREE * at + slot] = pieces_ref[block]
        return carry

    copies = []
    each = CHIPS // PICK_PARTS
    for part in range(PICK_PARTS):
        lax.fori_loop(part * each, (part + 1) * each, step, 0, unroll=True)
        at = pl.ds(part * each * FREE, each * FREE)
        copies.append(pltpu.make_async_copy(out_ref.at[at], out_hbm.at[at], sems.at[part]))
        copies[-1].start()
    for copy in copies:
        copy.wait()


def pick_pieces(listed, pieces, *ready):
    vmem = pl.BlockSpec(memory_space=pltpu.VMEM)
    shape = (CHIPS * FREE, PIECE, HD)
    return pl.pallas_call(
        pick_kernel,
        out_shape=jax.ShapeDtypeStruct(shape, jnp.bfloat16),
        in_specs=[pl.BlockSpec(memory_space=pltpu.SMEM), vmem] + [vmem] * len(ready),
        out_specs=pl.BlockSpec(memory_space=pltpu.HBM),
        scratch_shapes=[pltpu.VMEM(shape, jnp.bfloat16), pltpu.SemaphoreType.DMA((PICK_PARTS,))],
        cost_estimate=pl.CostEstimate(flops=0, bytes_accessed=1 << 20, transcendentals=0),
        compiler_params=pltpu.CompilerParams(vmem_limit_bytes=2 << 20),
    )(listed, pieces, *ready)


def head_rows(step):
    return slice(step * ROWS, (step + 1) * ROWS)


def listed_scores(step, q_ref, far_ref, bias):
    part, head = divmod(step, HEADS)
    q = q_ref[part * ROWS:(part + 1) * ROWS, head * HD:(head + 1) * HD]
    return dot_t(q, far_ref[:far_ref.shape[0] // 2, :]) + bias


def half_kernel(bias_ref, q_ref, far_ref, ml_ref, scores_ref, weights_ref, top_ref):
    bias = bias_ref[0:1, :]
    steps = HALF // ROWS * HEADS
    later = listed_scores(0, q_ref, far_ref, bias)
    for step in range(steps):
        part, head = divmod(step, HEADS)
        rows = slice(part * ROWS, (part + 1) * ROWS)
        scores = later
        later = listed_scores(step + 1, q_ref, far_ref, bias) if step + 1 < steps else None
        if step < AHEAD:
            m = jnp.maximum(jnp.max(scores, axis=1, keepdims=True), ml_ref[rows, head:head + 1])
            weights_ref[head_rows(step), :] = jnp.exp2((scores - m) * SCALE).astype(jnp.bfloat16)
            top_ref[rows, head:head + 1] = m
        else:
            scores_ref[head_rows(step - AHEAD), :] = scores


def half_scores(bias, queries, far, ml):
    vmem = pl.BlockSpec(memory_space=pltpu.VMEM)
    rows = AHEAD * ROWS
    return pl.pallas_call(
        half_kernel,
        out_shape=(
            pltpu.VMEM((HEADS * HALF - rows, 2 * HALF), jnp.float32),
            pltpu.VMEM((rows, 2 * HALF), jnp.bfloat16),
            pltpu.VMEM((HALF, HEADS), jnp.float32),
        ),
        in_specs=[vmem] * 4,
        out_specs=[vmem] * 3,
        cost_estimate=pl.CostEstimate(
            flops=2 * 2048 * 1024 * 128, bytes_accessed=1 << 20, transcendentals=rows * 1024
        ),
        compiler_params=pltpu.CompilerParams(vmem_limit_bytes=12 << 20),
    )(bias, queries, far, ml)


def far_kernel(bias_ref, q_ref, half_ref, weights_ref, top_ref, far_ref, farx_ref, acc_ref, ml_ref, w_hbm, out_hbm, att_ref, out_ref, w_ref, sems, w_sem):
    w_copy = pltpu.make_async_copy(w_hbm, w_ref, w_sem)
    w_copy.start()
    keys = 2 * HALF
    width = w_ref.shape[1]
    bias = bias_ref[0:1, :]
    vs = [with_ones(ref[keys:, :]) for ref in (far_ref, farx_ref)]
    copies = []

    def scores_of(step):
        there = listed_scores(step, q_ref, farx_ref, bias)
        return [there] if step < AHEAD else [half_ref[head_rows(step - AHEAD), :], there]

    def project(part):
        rows = slice(part * ROWS, (part + 1) * ROWS)
        if part == 0:
            w_copy.wait()
        for start in range(0, width, OUT_COLS):
            cols = slice(start, start + OUT_COLS)
            out_ref[rows, cols] = jnp.dot(
                att_ref[rows, :], w_ref[:, cols], preferred_element_type=jnp.float32
            ).astype(out_ref.dtype)
            at = (pl.ds(part * ROWS, ROWS), pl.ds(start, OUT_COLS))
            copies.append(
                pltpu.make_async_copy(out_ref.at[at], out_hbm.at[at], sems.at[len(copies)])
            )
            copies[-1].start()

    parts = HALF // ROWS
    later = scores_of(0)
    for step in range(parts * HEADS):
        part, head = divmod(step, HEADS)
        rows = slice(part * ROWS, (part + 1) * ROWS)
        scores = later
        later = scores_of(step + 1) if step + 1 < parts * HEADS else None
        if head == 0 and part > 0:
            project(part - 1)
        old = ml_ref[rows, head:head + 1]
        seen = top_ref[rows, head:head + 1] if step < AHEAD else old
        top = functools.reduce(jnp.maximum, scores)
        m = jnp.maximum(jnp.max(top, axis=1, keepdims=True), seen)
        keep = jnp.exp2((old - m) * SCALE)
        out = weighted(scores, vs[-len(scores):], m)
        if step < AHEAD:
            here = jnp.dot(
                weights_ref[head_rows(step), :], vs[0], preferred_element_type=jnp.float32
            )
            out = out + jnp.exp2((seen - m) * SCALE) * here
        total = out[:, HD:] + keep * ml_ref[rows, HEADS + head:HEADS + head + 1]
        top = out[:, :HD] + keep * acc_ref[rows, head * HD:(head + 1) * HD]
        att_ref[rows, head * HD:(head + 1) * HD] = (top / total).astype(jnp.bfloat16)
    project(parts - 1)
    for copy in copies:
        copy.wait()


def far_groups(bias, queries, half, far, far_pair, acc, ml, out_weight):
    width = out_weight.shape[1]
    vmem = pl.BlockSpec(memory_space=pltpu.VMEM)
    return pl.pallas_call(
        far_kernel,
        out_shape=jax.ShapeDtypeStruct((HALF, width), jnp.bfloat16),
        in_specs=[vmem] * 9
        + [pl.BlockSpec(memory_space=pltpu.HBM)],
        out_specs=pl.BlockSpec(memory_space=pltpu.HBM),
        scratch_shapes=[
            pltpu.VMEM((HALF, HEADS * HD), jnp.bfloat16),
            pltpu.VMEM((HALF, width), jnp.bfloat16),
            pltpu.VMEM(out_weight.shape, jnp.bfloat16),
            pltpu.SemaphoreType.DMA((HALF // ROWS * (width // OUT_COLS),)),
            pltpu.SemaphoreType.DMA,
        ],
        cost_estimate=pl.CostEstimate(
            flops=4 * 2 * 2048 * 2048 * 128 + 2 * 512 * 512 * 4096,
            bytes_accessed=12 << 20,
            transcendentals=2048 * 2048,
        ),
        compiler_params=pltpu.CompilerParams(vmem_limit_bytes=20 << 20),
    )(bias, queries, *half, far, far_pair, acc, ml, in_hbm(out_weight))


def swap_cores(value):
    return lax.ppermute(value, "core", [(0, 1), (1, 0)])


def local(queries, keys, values, selected, out_weight):
    listed = selected.T
    own, table = join(keys, values, listed)
    pieces = lax.all_to_all(
        own.reshape(CHIPS, PIECE, HD), CHIP_AXES, split_axis=0, concat_axis=0, tiled=True
    )
    near = lax.ppermute(own, CHIP_AXES, [(i, (i + 1) % CHIPS) for i in range(CHIPS)])
    near_pair = swap_cores(near)
    own_pair = swap_cores(own)
    outgoing = pick_pieces(table, pieces, own_pair, near, near_pair)
    far = lax.all_to_all(outgoing, CHIP_AXES, split_axis=0, concat_axis=0, tiled=True)
    far = far.reshape(CHIPS * FREE * PIECE, HD)
    acc, ml, queries, bias = near_groups(table, queries, own, own_pair, near, near_pair)
    far, acc, ml = lax.optimization_barrier((far, acc, ml))
    far_pair = swap_cores(far)
    half = half_scores(bias, queries, far, ml)
    return far_groups(bias, queries, half, far, far_pair, acc, ml, out_weight)


def solution(mesh):
    outer, inner = mesh.devices.shape
    fine = Mesh(mesh.devices.reshape(outer, inner // 2, 2), ALL_AXES)
    tokens = P(ALL_AXES, None)
    return jax.shard_map(
        local,
        mesh=fine,
        in_specs=(tokens, tokens, tokens, P(), P()),
        out_specs=tokens,
        check_vma=False,
    )
```

```python
import functools
import math

import jax
import jax.numpy as jnp
from jax import lax
from jax.experimental import pallas as pl
from jax.experimental.pallas import tpu as pltpu
from jax.sharding import Mesh
from jax.sharding import PartitionSpec as P

HEADS = 4
HD = 128
HALF = 512
CHIPS = 128
PIECE = 8
FREE = 2
LOG2E = 1.4426950408889634
SCALE = LOG2E / math.sqrt(HD)
NEG = -1e30
ROWS = 256
OUT_COLS = 1024
PICK_PARTS = 8
JOIN_PARTS = 4
AHEAD = 4
CHIP_AXES = ("outer", "ring")
ALL_AXES = ("outer", "ring", "core")


def dot_t(a, b):
    return lax.dot_general(a, b, (((1,), (1,)), ((), ())), preferred_element_type=jnp.float32)


def with_ones(values):
    return jnp.concatenate([values, jnp.ones_like(values)], axis=1)


def weighted(scores, values, m):
    out = None
    for s, v in zip(scores, values):
        p = jnp.exp2((s - m) * SCALE).astype(jnp.bfloat16)
        term = jnp.dot(p, v, preferred_element_type=jnp.float32)
        out = term if out is None else out + term
    return out


def in_hbm(array):
    return pltpu.with_memory_space_constraint(array, pltpu.HBM)


def near_kernel(listed_ref, q_hbm, own_ref, pair_ref, nb_ref, nbx_ref, acc_ref, ml_ref, q_ref, bias_ref, sem):
    q_copy = pltpu.make_async_copy(q_hbm, q_ref, sem)
    q_copy.start()
    block = lax.axis_index(CHIP_AXES)
    core = lax.axis_index("core")
    parity = (lax.broadcasted_iota(jnp.int32, (8, 2 * HALF), 1) // PIECE) % FREE
    bias_ref[...] = jnp.where(
        parity == 0,
        jnp.where(listed_ref[1, block] >= 0, 0.0, NEG),
        jnp.where(listed_ref[2, block] >= 0, 0.0, NEG),
    )
    own_bias = jnp.where(core == 1, 0.0, NEG)
    near_bias = jnp.where(block >= 1, 0.0, NEG)
    row_ids = lax.broadcasted_iota(jnp.int32, (ROWS, HALF), 0)
    col_ids = lax.broadcasted_iota(jnp.int32, (ROWS, HALF), 1)
    vs = [with_ones(ref[HALF:, :]) for ref in (own_ref, pair_ref, nb_ref, nbx_ref)]
    q_copy.wait()

    def scores_of(step):
        part, head = divmod(step, HEADS)
        q = q_ref[part * ROWS:(part + 1) * ROWS, head * HD:(head + 1) * HD]
        own = jnp.where(
            col_ids <= row_ids + part * ROWS, dot_t(q, own_ref[:HALF, :]), NEG
        )
        return [
            own,
            dot_t(q, pair_ref[:HALF, :]) + own_bias,
            dot_t(q, nb_ref[:HALF, :]) + near_bias,
            dot_t(q, nbx_ref[:HALF, :]) + near_bias,
        ]

    steps = HALF // ROWS * HEADS
    later = scores_of(0)
    for step in range(steps):
        part, head = divmod(step, HEADS)
        rows = slice(part * ROWS, (part + 1) * ROWS)
        scores = later
        later = scores_of(step + 1) if step + 1 < steps else None
        m = jnp.max(functools.reduce(jnp.maximum, scores), axis=1, keepdims=True)
        out = weighted(scores, vs, m)
        acc_ref[rows, head * HD:(head + 1) * HD] = out[:, :HD]
        ml_ref[rows, head:head + 1] = m
        ml_ref[rows, HEADS + head:HEADS + head + 1] = out[:, HD:HD + 1]


def near_groups(listed, queries, own, pair, near, near_pair):
    vmem = pl.BlockSpec(memory_space=pltpu.VMEM)
    return pl.pallas_call(
        near_kernel,
        out_shape=(
            pltpu.VMEM((HALF, HEADS * HD), jnp.float32),
            pltpu.VMEM((HALF, 2 * HEADS), jnp.float32),
            pltpu.VMEM(queries.shape, queries.dtype),
            pltpu.VMEM((8, 2 * HALF), jnp.float32),
        ),
        in_specs=[
            pl.BlockSpec(memory_space=pltpu.SMEM),
            pl.BlockSpec(memory_space=pltpu.HBM),
        ]
        + [vmem] * 4,
        out_specs=[vmem] * 4,
        scratch_shapes=[pltpu.SemaphoreType.DMA],
        cost_estimate=pl.CostEstimate(
            flops=4 * 2 * 2048 * 2048 * 128, bytes_accessed=4 << 20, transcendentals=2048 * 2048
        ),
        compiler_params=pltpu.CompilerParams(vmem_limit_bytes=20 << 20),
    )(listed, in_hbm(queries), own, pair, near, near_pair)


def join_kernel(keys_ref, values_ref, listed_ref, out_ref, table_ref, held_ref, sems):
    rows = keys_ref.shape[0]
    each = rows // JOIN_PARTS
    inward, outward = [], []
    for at, ref in enumerate((keys_ref, values_ref)):
        for part in range(JOIN_PARTS):
            here = pl.ds(at * rows + part * each, each)
            number = at * JOIN_PARTS + part
            inward.append(
                pltpu.make_async_copy(
                    ref.at[pl.ds(part * each, each)], held_ref.at[here], sems.at[0, number]
                )
            )
            outward.append(
                pltpu.make_async_copy(held_ref.at[here], out_ref.at[here], sems.at[1, number])
            )
    table = pltpu.make_async_copy(listed_ref, table_ref, sems.at[0, 2 * JOIN_PARTS])
    for copy in inward:
        copy.start()
    table.start()
    for first, second in zip(inward, outward):
        first.wait()
        second.start()
    for copy in outward:
        copy.wait()
    table.wait()


def join(keys, values, listed):
    hbm = pl.BlockSpec(memory_space=pltpu.HBM)
    shape = (2 * keys.shape[0], keys.shape[1])
    return pl.pallas_call(
        join_kernel,
        out_shape=(
            jax.ShapeDtypeStruct(shape, keys.dtype),
            pltpu.SMEM(listed.shape, listed.dtype),
        ),
        in_specs=[hbm] * 3,
        out_specs=(hbm, pl.BlockSpec(memory_space=pltpu.SMEM)),
        scratch_shapes=[
            pltpu.VMEM(shape, keys.dtype),
            pltpu.SemaphoreType.DMA((2, 2 * JOIN_PARTS + 1)),
        ],
        compiler_params=pltpu.CompilerParams(vmem_limit_bytes=2 << 20),
    )(in_hbm(keys), in_hbm(values), in_hbm(listed))


def pick_kernel(listed_ref, pieces_ref, *rest):
    out_hbm, out_ref, sems = rest[-3:]

    def step(at, carry):
        for slot in range(FREE):
            block = jnp.maximum(listed_ref[1 + slot, at], 0)
            out_ref[FREE * at + slot] = pieces_ref[block]
        return carry

    copies = []
    each = CHIPS // PICK_PARTS
    for part in range(PICK_PARTS):
        lax.fori_loop(part * each, (part + 1) * each, step, 0, unroll=True)
        at = pl.ds(part * each * FREE, each * FREE)
        copies.append(pltpu.make_async_copy(out_ref.at[at], out_hbm.at[at], sems.at[part]))
        copies[-1].start()
    for copy in copies:
        copy.wait()


def pick_pieces(listed, pieces, *ready):
    vmem = pl.BlockSpec(memory_space=pltpu.VMEM)
    shape = (CHIPS * FREE, PIECE, HD)
    return pl.pallas_call(
        pick_kernel,
        out_shape=jax.ShapeDtypeStruct(shape, jnp.bfloat16),
        in_specs=[pl.BlockSpec(memory_space=pltpu.SMEM), vmem] + [vmem] * len(ready),
        out_specs=pl.BlockSpec(memory_space=pltpu.HBM),
        scratch_shapes=[pltpu.VMEM(shape, jnp.bfloat16), pltpu.SemaphoreType.DMA((PICK_PARTS,))],
        cost_estimate=pl.CostEstimate(flops=0, bytes_accessed=1 << 20, transcendentals=0),
        compiler_params=pltpu.CompilerParams(vmem_limit_bytes=2 << 20),
    )(listed, pieces, *ready)


def head_rows(step):
    return slice(step * ROWS, (step + 1) * ROWS)


def listed_scores(step, q_ref, far_ref, bias):
    part, head = divmod(step, HEADS)
    q = q_ref[part * ROWS:(part + 1) * ROWS, head * HD:(head + 1) * HD]
    return dot_t(q, far_ref[:far_ref.shape[0] // 2, :]) + bias


def half_kernel(bias_ref, q_ref, far_ref, ml_ref, scores_ref, weights_ref, top_ref):
    bias = bias_ref[0:1, :]
    steps = HALF // ROWS * HEADS
    later = listed_scores(0, q_ref, far_ref, bias)
    for step in range(steps):
        part, head = divmod(step, HEADS)
        rows = slice(part * ROWS, (part + 1) * ROWS)
        scores = later
        later = listed_scores(step + 1, q_ref, far_ref, bias) if step + 1 < steps else None
        if step < AHEAD:
            m = jnp.maximum(jnp.max(scores, axis=1, keepdims=True), ml_ref[rows, head:head + 1])
            weights_ref[head_rows(step), :] = jnp.exp2((scores - m) * SCALE).astype(jnp.bfloat16)
            top_ref[rows, head:head + 1] = m
        else:
            scores_ref[head_rows(step - AHEAD), :] = scores


def half_scores(bias, queries, far, ml):
    vmem = pl.BlockSpec(memory_space=pltpu.VMEM)
    rows = AHEAD * ROWS
    return pl.pallas_call(
        half_kernel,
        out_shape=(
            pltpu.VMEM((HEADS * HALF - rows, 2 * HALF), jnp.float32),
            pltpu.VMEM((rows, 2 * HALF), jnp.bfloat16),
            pltpu.VMEM((HALF, HEADS), jnp.float32),
        ),
        in_specs=[vmem] * 4,
        out_specs=[vmem] * 3,
        cost_estimate=pl.CostEstimate(
            flops=2 * 2048 * 1024 * 128, bytes_accessed=1 << 20, transcendentals=rows * 1024
        ),
        compiler_params=pltpu.CompilerParams(vmem_limit_bytes=12 << 20),
    )(bias, queries, far, ml)


def far_kernel(bias_ref, q_ref, half_ref, weights_ref, top_ref, far_ref, farx_ref, acc_ref, ml_ref, w_hbm, out_hbm, att_ref, out_ref, w_ref, sems, w_sem):
    w_copy = pltpu.make_async_copy(w_hbm, w_ref, w_sem)
    w_copy.start()
    keys = 2 * HALF
    width = w_ref.shape[1]
    bias = bias_ref[0:1, :]
    vs = [with_ones(ref[keys:, :]) for ref in (far_ref, farx_ref)]
    copies = []

    def scores_of(step):
        there = listed_scores(step, q_ref, farx_ref, bias)
        return [there] if step < AHEAD else [half_ref[head_rows(step - AHEAD), :], there]

    def project(part):
        rows = slice(part * ROWS, (part + 1) * ROWS)
        if part == 0:
            w_copy.wait()
        for start in range(0, width, OUT_COLS):
            cols = slice(start, start + OUT_COLS)
            out_ref[rows, cols] = jnp.dot(
                att_ref[rows, :], w_ref[:, cols], preferred_element_type=jnp.float32
            ).astype(out_ref.dtype)
            at = (pl.ds(part * ROWS, ROWS), pl.ds(start, OUT_COLS))
            copies.append(
                pltpu.make_async_copy(out_ref.at[at], out_hbm.at[at], sems.at[len(copies)])
            )
            copies[-1].start()

    parts = HALF // ROWS
    later = scores_of(0)
    for step in range(parts * HEADS):
        part, head = divmod(step, HEADS)
        rows = slice(part * ROWS, (part + 1) * ROWS)
        scores = later
        later = scores_of(step + 1) if step + 1 < parts * HEADS else None
        if head == 0 and part > 0:
            project(part - 1)
        old = ml_ref[rows, head:head + 1]
        seen = top_ref[rows, head:head + 1] if step < AHEAD else old
        top = functools.reduce(jnp.maximum, scores)
        m = jnp.maximum(jnp.max(top, axis=1, keepdims=True), seen)
        keep = jnp.exp2((old - m) * SCALE)
        out = weighted(scores, vs[-len(scores):], m)
        if step < AHEAD:
            here = jnp.dot(
                weights_ref[head_rows(step), :], vs[0], preferred_element_type=jnp.float32
            )
            out = out + jnp.exp2((seen - m) * SCALE) * here
        total = out[:, HD:] + keep * ml_ref[rows, HEADS + head:HEADS + head + 1]
        top = out[:, :HD] + keep * acc_ref[rows, head * HD:(head + 1) * HD]
        att_ref[rows, head * HD:(head + 1) * HD] = (top / total).astype(jnp.bfloat16)
    project(parts - 1)
    for copy in copies:
        copy.wait()


def far_groups(bias, queries, half, far, far_pair, acc, ml, out_weight):
    width = out_weight.shape[1]
    vmem = pl.BlockSpec(memory_space=pltpu.VMEM)
    return pl.pallas_call(
        far_kernel,
        out_shape=jax.ShapeDtypeStruct((HALF, width), jnp.bfloat16),
        in_specs=[vmem] * 9
        + [pl.BlockSpec(memory_space=pltpu.HBM)],
        out_specs=pl.BlockSpec(memory_space=pltpu.HBM),
        scratch_shapes=[
            pltpu.VMEM((HALF, HEADS * HD), jnp.bfloat16),
            pltpu.VMEM((HALF, width), jnp.bfloat16),
            pltpu.VMEM(out_weight.shape, jnp.bfloat16),
            pltpu.SemaphoreType.DMA((HALF // ROWS * (width // OUT_COLS),)),
            pltpu.SemaphoreType.DMA,
        ],
        cost_estimate=pl.CostEstimate(
            flops=4 * 2 * 2048 * 2048 * 128 + 2 * 512 * 512 * 4096,
            bytes_accessed=12 << 20,
            transcendentals=2048 * 2048,
        ),
        compiler_params=pltpu.CompilerParams(vmem_limit_bytes=20 << 20),
    )(bias, queries, *half, far, far_pair, acc, ml, in_hbm(out_weight))


def swap_cores(value):
    return lax.ppermute(value, "core", [(0, 1), (1, 0)])


def local(queries, keys, values, selected, out_weight):
    listed = selected.T
    own, table = join(keys, values, listed)
    pieces = lax.all_to_all(
        own.reshape(CHIPS, PIECE, HD), CHIP_AXES, split_axis=0, concat_axis=0, tiled=True
    )
    near = lax.ppermute(own, CHIP_AXES, [(i, (i + 1) % CHIPS) for i in range(CHIPS)])
    near_pair = swap_cores(near)
    own_pair = swap_cores(own)
    outgoing = pick_pieces(table, pieces, own_pair, near, near_pair)
    far = lax.all_to_all(outgoing, CHIP_AXES, split_axis=0, concat_axis=0, tiled=True)
    far = far.reshape(CHIPS * FREE * PIECE, HD)
    acc, ml, queries, bias = near_groups(table, queries, own, own_pair, near, near_pair)
    far, acc, ml = lax.optimization_barrier((far, acc, ml))
    far_pair = swap_cores(far)
    half = half_scores(bias, queries, far, ml)
    return far_groups(bias, queries, half, far, far_pair, acc, ml, out_weight)


def solution(mesh):
    outer, inner = mesh.devices.shape
    fine = Mesh(mesh.devices.reshape(outer, inner // 2, 2), ALL_AXES)
    tokens = P(ALL_AXES, None)
    return jax.shard_map(
        local,
        mesh=fine,
        in_specs=(tokens, tokens, tokens, P(), P()),
        out_specs=tokens,
        check_vma=False,
    )
```
